32 devices in a mesh: seg: 8 (over z, y), grp: 4 (over x, core).
Axes of the slice: x: 2, y: 2, z: 4, core: 2. Of those that a mesh axis runs over, the one named last changes fastest.
Arguments:
- spectra: bfloat16 [8, 2, 128, 12288], P(None, None, None, ('seg', 'grp'))
- band_bins: int32 [2, 2], replicated, may hold values from 0 to 80, as said below
- far_list: int32 [4, 8, 8, 4, 3], P('grp'), may hold values from 0 to 2, as said below
- far_count: int32 [4, 8, 8], P('grp'), may hold values from 0 to 4, as said below
Outputs:
- near_corr: bfloat16 [2, 2, 12288, 1536], P(None, None, ('seg', 'grp'))
- far_corr: bfloat16 [8, 4, 8, 4, 2, 128, 128], P('seg', 'grp')
The draws below stay inside these ranges and needn't reach their ends.
Inputs may be any that keep to these rules, and one draw needn't show every extreme that they name: band_bins[b, 0] + 48 <= 128 and 1 <= band_bins[b, 1] <= 48; band 0 has exactly 48 bins; one band starts at bin 0 and the other at bin 128 - 48. far_list entries: row and column blocks 0 to 2, band 0 or 1. far_count is 0 where owner and source group are the same; every owner has some source group with exactly 4.
All inputs are finite; a program needn't handle non-finite values.
Results may differ from the reference program's by a relative error of at most 0.0058.
Values may be sent and summed in bfloat16 or wider, within the bound.
A program may use at most 192 MiB of HBM per device.

```python
import math
import jax
import jax.numpy as jnp
from jax import lax

W = 8
F = 128
BAND_MAX = 48
SMOOTH = 4
BLOCK = 128
BLK_DEV = 3
CAP = 4
SEGS = 8
GRPS = 4
NBLK = 96
NCH = 12288
GCH = 1536
DEVICES = 32


def draw_spectra(key, part):
    key_amp = jax.random.fold_in(key, 11)
    key_gain = jax.random.fold_in(key, 12)
    key_noise = jax.random.fold_in(key, 13)
    amplitude = jnp.exp(jax.random.uniform(key_amp, (F, NCH), jnp.float32, math.log(0.1), math.log(10.0)))
    gains = jax.random.uniform(key_gain, (W, NCH), jnp.float32, 0.5, 2.0)
    noise = jax.random.normal(key_noise, (W, 2, F, NCH), jnp.float32)
    values = noise * amplitude[None, None] * gains[:, None, None, :]
    return values.astype(jnp.bfloat16)


def draw_band_bins(key, part):
    key_start = jax.random.fold_in(key, 21)
    key_count = jax.random.fold_in(key, 22)
    flip = jax.random.randint(key_start, (1,), 0, 2, jnp.int32)
    first = flip * (F - BAND_MAX)
    other = (1 - flip) * (F - BAND_MAX)
    starts = jnp.concatenate([first, other])
    second = jax.random.randint(key_count, (1,), BAND_MAX // 2 + 1, BAND_MAX + 1, jnp.int32)
    counts = jnp.concatenate([jnp.full((1,), BAND_MAX, jnp.int32), second])
    return jnp.stack([starts, counts], axis=1).astype(jnp.int32)


def draw_far_list(key, part):
    key_row = jax.random.fold_in(key, 31)
    key_col = jax.random.fold_in(key, 32)
    key_band = jax.random.fold_in(key, 33)
    shape = (GRPS, SEGS, SEGS, CAP)
    rows = jax.random.randint(key_row, shape, 0, BLK_DEV, jnp.int32)
    cols = jax.random.randint(key_col, shape, 0, BLK_DEV, jnp.int32)
    bands = jax.random.randint(key_band, shape, 0, 2, jnp.int32)
    return jnp.stack([rows, cols, bands], axis=-1)


def draw_far_count(key, part):
    key_base = jax.random.fold_in(key, 41)
    key_full = jax.random.fold_in(key, 42)
    shape = (GRPS, SEGS, SEGS)
    base = jax.random.randint(key_base, shape, 0, CAP + 1, jnp.int32)
    owner = jax.lax.broadcasted_iota(jnp.int32, shape, 1)
    source = jax.lax.broadcasted_iota(jnp.int32, shape, 2)
    pick = jax.random.randint(key_full, (GRPS, SEGS), 0, SEGS - 1, jnp.int32)
    owner_two = jax.lax.broadcasted_iota(jnp.int32, (GRPS, SEGS), 1)
    pick = pick + (pick >= owner_two).astype(jnp.int32)
    full = source == pick[:, :, None]
    counts = jnp.where(full, CAP, base)
    return jnp.where(owner == source, 0, counts).astype(jnp.int32)


def setup_inputs(seed: int = 0) -> dict:
    keys = jax.random.split(jax.random.key(seed), 5)
    return {
        "spectra": draw_spectra(jax.random.fold_in(keys[4], 71), 0),
        "band_bins": draw_band_bins(jax.random.fold_in(keys[4], 71), 0),
        "far_list": draw_far_list(jax.random.fold_in(keys[4], 71), 0),
        "far_count": draw_far_count(jax.random.fold_in(keys[4], 71), 0),
    }


HIGH = lax.Precision.HIGHEST

def whiten(spectra):
    values = spectra.astype(jnp.float32)
    power = lax.optimization_barrier(jnp.sum(values * values, axis=(0, 1)))
    bins = jnp.arange(F)
    window = (jnp.abs(bins[:, None] - bins[None, :]) <= SMOOTH).astype(jnp.float32)
    totals = lax.optimization_barrier(jnp.sum(window, axis=1)) * W
    level = jnp.dot(window, power, precision=HIGH, preferred_element_type=jnp.float32) / totals[:, None]
    return (values * lax.rsqrt(level + 1e-06)[None, None]).astype(jnp.bfloat16)

def band_operands(white, band_bins):
    cols = []
    ops = []
    for band in range(2):
        piece = lax.dynamic_slice_in_dim(white, band_bins[band, 0], BAND_MAX, 2)
        live = (jnp.arange(BAND_MAX) < band_bins[band, 1]).astype(jnp.bfloat16)
        rows = piece * live[None, None, :, None]
        twisted = jnp.stack([rows[:, 1], -rows[:, 0]], axis=1)
        cols.append(piece)
        ops.append(jnp.stack([rows, twisted], axis=0))
    scales = lax.rsqrt((W * band_bins[:, 1]).astype(jnp.float32))
    return (jnp.stack(cols), jnp.stack(ops), scales)

def reference(spectra, band_bins, far_list, far_count):
    white = whiten(spectra)
    band_cols, row_ops, scales = band_operands(white, band_bins)
    group_cols = band_cols.reshape(2, W, 2, BAND_MAX, SEGS, GCH)
    group_ops = row_ops.reshape(2, 2, W, 2, BAND_MAX, SEGS, GCH)

    def one_group(index):
        cols_here = lax.dynamic_index_in_dim(group_cols, index, 4, keepdims=False).astype(jnp.float32)
        ops_here = lax.dynamic_index_in_dim(group_ops, index, 5, keepdims=False).astype(jnp.float32)
        prod = jnp.einsum('bowpfr,bwpfk->bork', ops_here, cols_here)
        return (prod * scales[:, None, None, None]).astype(jnp.bfloat16)
    near = lax.map(one_group, jnp.arange(SEGS, dtype=jnp.int32))
    near_corr = jnp.transpose(near, (1, 2, 0, 3, 4)).reshape(2, 2, NCH, GCH)
    lists = jnp.transpose(far_list, (1, 0, 2, 3, 4))
    table = jnp.transpose(far_count, (1, 0, 2))
    shape = (SEGS, GRPS, SEGS, CAP)
    owner = lax.broadcasted_iota(jnp.int32, shape, 0)
    member = lax.broadcasted_iota(jnp.int32, shape, 1)
    source = lax.broadcasted_iota(jnp.int32, shape, 2)
    slot = lax.broadcasted_iota(jnp.int32, shape, 3)
    row_block = (owner * GRPS + member) * BLK_DEV + lists[..., 0]
    col_block = (source * GRPS + member) * BLK_DEV + lists[..., 1]
    band_pick = lists[..., 2]
    alive = (slot < table[..., None]).astype(jnp.float32)
    per_dev = SEGS * CAP
    row_block = row_block.reshape(DEVICES, per_dev)
    col_block = col_block.reshape(DEVICES, per_dev)
    band_pick = band_pick.reshape(DEVICES, per_dev)
    alive = alive.reshape(DEVICES, per_dev)
    block_cols = band_cols.reshape(2, W, 2, BAND_MAX, NBLK, BLOCK)
    block_ops = row_ops.reshape(2, 2, W, 2, BAND_MAX, NBLK, BLOCK)

    def one_owner(inputs):
        rows_i, cols_i, bands_i, alive_i = inputs
        chosen_cols = block_cols[bands_i, :, :, :, cols_i, :].astype(jnp.float32)
        chosen_ops = block_ops[bands_i, :, :, :, :, rows_i, :].astype(jnp.float32)
        prod = jnp.einsum('cowpfr,cwpfk->cork', chosen_ops, chosen_cols)
        factor = scales[bands_i] * alive_i
        return (prod * factor[:, None, None, None]).astype(jnp.bfloat16)
    far = lax.map(one_owner, (row_block, col_block, band_pick, alive))
    far_corr = far.reshape(SEGS, GRPS, SEGS, CAP, 2, BLOCK, BLOCK)
    return (near_corr, far_corr)
```

```python
import functools

import jax
import jax.numpy as jnp
from jax import lax
from jax.experimental import pallas as pl
from jax.experimental.pallas import tpu as pltpu
from jax.sharding import PartitionSpec as P

W = 8
F = 128
BAND_MAX = 48
SMOOTH = 4
BLOCK = 128
BLK_DEV = 3
DEPTH = W * 2 * BAND_MAX
PIECES = 2 * BLK_DEV
LINE_Z = 4
CORES = 2


HIGH = lax.Precision.HIGHEST
MESH = pl.DeviceIdType.MESH


def whiten_gain(spectra):
    values = spectra.astype(jnp.float32)
    power = jnp.sum(values * values, axis=(0, 1))
    bins = jnp.arange(F)
    window = (jnp.abs(bins[:, None] - bins[None, :]) <= SMOOTH).astype(jnp.float32)
    totals = jnp.sum(window, axis=1) * W
    level = (
        jnp.dot(window, power, precision=HIGH, preferred_element_type=jnp.float32) / totals[:, None]
    )
    return lax.rsqrt(level + 1e-06)


def band_operands(spectra, gain, band_bins):
    cols = []
    ops = []
    for band in range(2):
        start = band_bins[band, 0]
        values = lax.dynamic_slice_in_dim(spectra, start, BAND_MAX, 2).astype(jnp.float32)
        scale = lax.dynamic_slice_in_dim(gain, start, BAND_MAX, 0)
        piece = (values * scale[None, None]).astype(jnp.bfloat16)
        piece = piece.reshape(W, 2, BAND_MAX, BLK_DEV, BLOCK)
        live = (jnp.arange(BAND_MAX) < band_bins[band, 1]).astype(jnp.bfloat16)
        rows = piece * live[None, None, :, None, None]
        twisted = jnp.stack([rows[:, 1], -rows[:, 0]], axis=1)
        cols.append(jnp.transpose(piece.reshape(DEPTH, BLK_DEV, BLOCK), (1, 0, 2)))
        both = jnp.stack([rows, twisted], axis=0).reshape(2, DEPTH, BLK_DEV, BLOCK)
        ops.append(jnp.transpose(both, (2, 0, 3, 1)).reshape(BLK_DEV, 2 * BLOCK, DEPTH))
    scales = lax.rsqrt((W * band_bins[:, 1]).astype(jnp.float32))
    return (jnp.concatenate(cols), jnp.stack(ops), scales)


class Gather:
    def __init__(self, axis, high, low, own, buf, send, recv):
        self.axis, self.high, self.low = axis, high, low
        self.own, self.buf, self.send, self.recv = own, buf, send, recv
        self.me = lax.axis_index(axis)
        self.p, self.l = lax.div(self.me, low), lax.rem(self.me, low)
        p, l = self.p, self.l
        self.dirs = [
            (p + 1 < high, self.me + low),
            (p > 0, self.me - low),
            (l + 1 < low, self.me + 1),
            (l > 0, self.me - 1),
        ]
        if high == 1:
            self.dirs[0] = self.dirs[1] = None
        if low == 1:
            self.dirs[2] = self.dirs[3] = None
        self.closing = False

    def greet(self, barrier):
        for entry in self.dirs:
            if entry is not None:

                @pl.when(entry[0])
                def _():
                    pl.semaphore_signal(
                        barrier, inc=1, device_id={self.axis: entry[1]}, device_id_type=MESH
                    )

    def peers(self):
        return sum(jnp.where(entry[0], 1, 0) for entry in self.dirs if entry is not None)

    def copy(self, way, src, q, own):
        return pltpu.make_async_remote_copy(
            src_ref=self.own.at[q] if own else self.buf.at[src, q],
            dst_ref=self.buf.at[src, q],
            send_sem=self.send.at[way, src, q],
            recv_sem=self.recv.at[src, q],
            device_id={self.axis: self.dirs[way][1]},
            device_id_type=MESH,
        )

    def pass_on(self, ways, src, q, own=False):
        for way in ways:
            if self.dirs[way] is not None:

                @pl.when(self.dirs[way][0])
                def _():
                    piece = self.copy(way, src, q, own)
                    if self.closing:
                        piece.wait_send()
                    else:
                        piece.start()

    def arrive(self, there, src, q, ways, use):
        @pl.when(there)
        def _():
            if not self.closing:
                pltpu.make_async_copy(
                    self.buf.at[src, q], self.buf.at[src, q], self.recv.at[src, q]
                ).wait()
            self.pass_on(ways, src, q)
            if use is not None and not self.closing:
                use(src, q)

    def start(self, q):
        self.pass_on((0, 1, 2, 3), self.me, q, own=True)

    def step(self, st, q, use):
        p, l, low = self.p, self.l, self.low
        if 0 < st < self.high:
            self.arrive(p - st >= 0, (p - st) * low + l, q, (0, 2, 3), use)
            self.arrive(p + st < self.high, (p + st) * low + l, q, (1, 2, 3), use)
        d = st - 1
        if 0 <= d < self.high:
            for far in [p] if d == 0 else [p - d, p + d]:
                inside = (far >= 0) & (far < self.high)
                for e in range(1, low):
                    self.arrive(inside & (l - e >= 0), far * low + l - e, q, (2,), use)
                    self.arrive(inside & (l + e < low), far * low + l + e, q, (3,), use)


def kernel(
    nseg, ngrp, lists, factors, scales, cols, ops, near, far, seg_buf, grp_buf,
    seg_send, seg_recv, grp_send, grp_recv, move,
):
    seg = Gather("seg", LINE_Z, nseg // LINE_Z, cols, seg_buf, seg_send, seg_recv)
    grp = Gather("grp", ngrp // CORES, CORES, cols, grp_buf, grp_send, grp_recv)
    barrier = pltpu.get_barrier_semaphore()
    seg.greet(barrier)
    grp.greet(barrier)
    pl.semaphore_wait(barrier, seg.peers() + grp.peers())

    def loop(fn):
        def step(q, carry):
            fn(q)
            return carry

        lax.fori_loop(0, PIECES, step, 0)

    def near_from(piece, src, q):
        band, m = lax.div(q, BLK_DEV), lax.rem(q, BLK_DEV)
        at = pl.ds(pl.multiple_of(src * (BLK_DEV * BLOCK) + m * BLOCK, BLOCK), BLOCK)
        for i in range(BLK_DEV):
            prod = jnp.dot(ops[band, i], piece, preferred_element_type=jnp.float32)
            prod = (prod * scales[band]).astype(jnp.bfloat16)
            near[band, 0, i * BLOCK : (i + 1) * BLOCK, at] = prod[:BLOCK]
            near[band, 1, i * BLOCK : (i + 1) * BLOCK, at] = prod[BLOCK:]

    def use_near(src, q):
        near_from(grp_buf[src, q], src, q)

    def begin(q):
        seg.start(q)
        grp.start(q)

    loop(begin)
    loop(lambda q: near_from(cols[q], grp.me, q))

    def steps():
        for st in range(1, max(seg.high, grp.high) + 1):

            def both(q):
                seg.step(st, q, None)
                grp.step(st, q, use_near)

            loop(both)

    steps()

    own = pltpu.make_async_copy(cols, seg_buf.at[seg.me], move)
    own.start()
    own.wait()

    def far_source(t, carry):
        for c in range(lists.shape[1] // 3):
            i, m, band = lists[t, 3 * c], lists[t, 3 * c + 1], lists[t, 3 * c + 2]
            prod = jnp.dot(
                ops[band, i], seg_buf[t, band * BLK_DEV + m], preferred_element_type=jnp.float32
            )
            prod = (prod * factors[t, c]).astype(jnp.bfloat16)
            far[t, c, 0] = prod[:BLOCK]
            far[t, c, 1] = prod[BLOCK:]
        return carry

    lax.fori_loop(0, nseg, far_source, 0)

    seg.closing = grp.closing = True
    loop(begin)
    steps()


def body(nseg, ngrp, spectra, band_bins, far_list, far_count):
    gain = whiten_gain(spectra)
    cols, ops, scales = band_operands(spectra, gain, band_bins)
    seg_index = lax.axis_index("seg")
    taken = lax.dynamic_index_in_dim(far_list[0], seg_index, 0, keepdims=False)
    count = lax.dynamic_index_in_dim(far_count[0], seg_index, 0, keepdims=False)
    slots = taken.shape[1]
    live = (jnp.arange(slots)[None, :] < count[:, None]).astype(jnp.float32)
    factors = scales[taken[..., 2]] * live
    smem = pl.BlockSpec(memory_space=pltpu.SMEM)
    vmem = pl.BlockSpec(memory_space=pltpu.VMEM)
    sems = pltpu.SemaphoreType.DMA
    near, far = pl.pallas_call(
        functools.partial(kernel, nseg, ngrp),
        out_shape=(
            jax.ShapeDtypeStruct(
                (2, 2, BLK_DEV * BLOCK, ngrp * BLK_DEV * BLOCK), jnp.bfloat16
            ),
            jax.ShapeDtypeStruct((nseg, slots, 2, BLOCK, BLOCK), jnp.bfloat16),
        ),
        in_specs=[smem, smem, smem, vmem, vmem],
        out_specs=(vmem, vmem),
        scratch_shapes=[
            pltpu.VMEM((nseg, PIECES, DEPTH, BLOCK), jnp.bfloat16),
            pltpu.VMEM((ngrp, PIECES, DEPTH, BLOCK), jnp.bfloat16),
            sems((4, nseg, PIECES)),
            sems((nseg, PIECES)),
            sems((4, ngrp, PIECES)),
            sems((ngrp, PIECES)),
            sems,
        ],
        compiler_params=pltpu.CompilerParams(
            collective_id=0, has_side_effects=True, vmem_limit_bytes=56 * 1024 * 1024
        ),
    )(taken.reshape(nseg, slots * 3), factors, scales, cols, ops)
    return (near, far[None, None])


def solution(mesh):
    placed = (
        P(None, None, None, ("seg", "grp")),
        P(),
        P("grp", None, None, None, None),
        P("grp", None, None),
    )
    return jax.shard_map(
        functools.partial(body, mesh.shape["seg"], mesh.shape["grp"]),
        mesh=mesh,
        in_specs=placed,
        out_specs=(
            P(None, None, ("seg", "grp"), None),
            P("seg", "grp", None, None, None, None, None),
        ),
        check_vma=False,
    )
```

```python
import functools

import jax
import jax.numpy as jnp
from jax import lax
from jax.experimental import pallas as pl
from jax.experimental.pallas import tpu as pltpu
from jax.sharding import PartitionSpec as P

W = 8
F = 128
BAND_MAX = 48
SMOOTH = 4
BLOCK = 128
BLK_DEV = 3
DEPTH = W * 2 * BAND_MAX
PIECES = 2 * BLK_DEV
LINE_Z = 4
CORES = 2


HIGH = lax.Precision.HIGHEST
MESH = pl.DeviceIdType.MESH


def whiten_kernel(bins, spectra, cols, gain):
    power = jnp.zeros((F, BLOCK), jnp.float32)
    for w in range(W):
        for p in range(2):
            values = spectra[w, p].astype(jnp.float32)
            power = power + values * values
    f = lax.broadcasted_iota(jnp.int32, (F, F), 0)
    g = lax.broadcasted_iota(jnp.int32, (F, F), 1)
    window = jnp.where(jnp.abs(f - g) <= SMOOTH, 1.0, 0.0).astype(jnp.float32)
    totals = jnp.sum(window, axis=1, keepdims=True) * W
    level = jnp.dot(window, power, precision=HIGH, preferred_element_type=jnp.float32) / totals
    gain[...] = lax.rsqrt(level + 1e-06)
    for band in range(2):
        at = pl.ds(pl.multiple_of(bins[band, 0], 16), BAND_MAX)
        scale = gain[at]
        for p in range(2):
            for w in range(W):
                first = (p * W + w) * BAND_MAX
                piece = spectra[w, p, at].astype(jnp.float32) * scale
                cols[band, 0, first : first + BAND_MAX] = piece.astype(jnp.bfloat16)


def band_columns(spectra, band_bins):
    return pl.pallas_call(
        whiten_kernel,
        grid=(BLK_DEV,),
        out_shape=jax.ShapeDtypeStruct((2, BLK_DEV, DEPTH, BLOCK), jnp.bfloat16),
        in_specs=[
            pl.BlockSpec(memory_space=pltpu.SMEM),
            pl.BlockSpec((W, 2, F, BLOCK), lambda m: (0, 0, 0, m)),
        ],
        out_specs=pl.BlockSpec((2, 1, DEPTH, BLOCK), lambda m: (0, m, 0, 0)),
        scratch_shapes=[pltpu.VMEM((F, BLOCK), jnp.float32)],
        compiler_params=pltpu.CompilerParams(vmem_limit_bytes=56 * 1024 * 1024),
    )(band_bins, spectra).reshape(PIECES, DEPTH, BLOCK)


class Gather:
    def __init__(self, axis, high, low, own, buf, send, recv):
        self.axis, self.high, self.low = axis, high, low
        self.own, self.buf, self.send, self.recv = own, buf, send, recv
        self.me = lax.axis_index(axis)
        self.p, self.l = lax.div(self.me, low), lax.rem(self.me, low)
        p, l = self.p, self.l
        self.dirs = [
            (p + 1 < high, self.me + low),
            (p > 0, self.me - low),
            (l + 1 < low, self.me + 1),
            (l > 0, self.me - 1),
        ]
        if high == 1:
            self.dirs[0] = self.dirs[1] = None
        if low == 1:
            self.dirs[2] = self.dirs[3] = None
        self.closing = False

    def greet(self, barrier):
        for entry in self.dirs:
            if entry is not None:

                @pl.when(entry[0])
                def _():
                    pl.semaphore_signal(
                        barrier, inc=1, device_id={self.axis: entry[1]}, device_id_type=MESH
                    )

    def peers(self):
        return sum(jnp.where(entry[0], 1, 0) for entry in self.dirs if entry is not None)

    def copy(self, way, src, q, own):
        return pltpu.make_async_remote_copy(
            src_ref=self.own.at[q] if own else self.buf.at[src, q],
            dst_ref=self.buf.at[src, q],
            send_sem=self.send.at[way, src, q],
            recv_sem=self.recv.at[src, q],
            device_id={self.axis: self.dirs[way][1]},
            device_id_type=MESH,
        )

    def pass_on(self, ways, src, q, own=False):
        for way in ways:
            if self.dirs[way] is not None:

                @pl.when(self.dirs[way][0])
                def _():
                    piece = self.copy(way, src, q, own)
                    if self.closing:
                        piece.wait_send()
                    else:
                        piece.start()

    def arrive(self, there, src, q, ways, use):
        @pl.when(there)
        def _():
            if not self.closing:
                pltpu.make_async_copy(
                    self.buf.at[src, q], self.buf.at[src, q], self.recv.at[src, q]
                ).wait()
            self.pass_on(ways, src, q)
            if use is not None and not self.closing:
                use(src, q)

    def start(self, q):
        self.pass_on((0, 1, 2, 3), self.me, q, own=True)

    def step(self, st, q, use, low_first=False):
        p, l, low = self.p, self.l, self.low
        turn = () if low_first else (2, 3)
        if 0 < st < self.high:
            self.arrive(p - st >= 0, (p - st) * low + l, q, (0,) + turn, use)
            self.arrive(p + st < self.high, (p + st) * low + l, q, (1,) + turn, use)
        d = st - 1
        if not 0 <= d < self.high:
            return
        for far, way in [(p, None)] if d == 0 else [(p - d, 0), (p + d, 1)]:
            inside = (far >= 0) & (far < self.high)
            for e in range(1, low):
                for there, other, on in ((l - e >= 0, l - e, 2), (l + e < low, l + e, 3)):
                    if not low_first:
                        ways = (on,)
                    elif d == 0:
                        ways = (0, 1, on)
                    else:
                        ways = (way,)
                    self.arrive(inside & there, far * low + other, q, ways, use)


def kernel(
    nseg, ngrp, bins, lists, counts, cols, near, far, seg_buf, grp_buf, ops,
    seg_send, seg_recv, grp_send, grp_recv, move,
):
    seg = Gather("seg", LINE_Z, nseg // LINE_Z, cols, seg_buf, seg_send, seg_recv)
    grp = Gather("grp", ngrp // CORES, CORES, cols, grp_buf, grp_send, grp_recv)
    barrier = pltpu.get_barrier_semaphore()
    seg.greet(barrier)
    grp.greet(barrier)
    pl.semaphore_wait(barrier, seg.peers() + grp.peers())

    def loop(fn, first=0):
        def step(q, carry):
            fn(q)
            return carry

        lax.fori_loop(first, PIECES, step, 0)

    def begin(q):
        seg.start(q)
        grp.start(q)

    loop(begin)
    own = pltpu.make_async_copy(cols, seg_buf.at[seg.me], move)
    own.start()

    half = DEPTH // 2

    def operands(q):
        band, m = lax.div(q, BLK_DEV), lax.rem(q, BLK_DEV)
        bin_of = lax.rem(lax.broadcasted_iota(jnp.int32, (1, DEPTH), 1), BAND_MAX)
        live = jnp.where(bin_of < bins[band, 1], 1.0, 0.0).astype(jnp.float32)
        rows = jnp.transpose(cols[q].astype(jnp.float32)) * live
        ops[band, m, :BLOCK] = rows.astype(jnp.bfloat16)
        ops[band, m, BLOCK:, :half] = rows[:, half:].astype(jnp.bfloat16)
        ops[band, m, BLOCK:, half:] = (-rows[:, :half]).astype(jnp.bfloat16)

    loop(operands)

    def scale(band):
        return lax.rsqrt(jnp.full((1, BLOCK), W * bins[band, 1], jnp.int32).astype(jnp.float32))

    def near_from(piece, src, q):
        band, m = lax.div(q, BLK_DEV), lax.rem(q, BLK_DEV)
        at = pl.ds(pl.multiple_of(src * (BLK_DEV * BLOCK) + m * BLOCK, BLOCK), BLOCK)
        for i in range(BLK_DEV):
            prod = jnp.dot(ops[band, i], piece, preferred_element_type=jnp.float32)
            prod = (prod * scale(band)).astype(jnp.bfloat16)
            near[band, 0, i * BLOCK : (i + 1) * BLOCK, at] = prod[:BLOCK]
            near[band, 1, i * BLOCK : (i + 1) * BLOCK, at] = prod[BLOCK:]

    def use_near(src, q):
        near_from(grp_buf[src, q], src, q)

    loop(lambda q: near_from(cols[q], grp.me, q))

    def steps():
        for st in range(1, max(seg.high, grp.high) + 1):

            def both(q, low_first=False):
                seg.step(st, q, None, low_first)
                grp.step(st, q, use_near)

            both(jnp.int32(0), low_first=True)
            loop(both, 1)

    steps()
    own.wait()

    slots = far.shape[1]

    def far_source(t, carry):
        for c in range(slots):
            entry = (t * slots + c) * 3
            i = lists[seg.me, entry]
            m = lists[seg.me, entry + 1]
            band = lists[seg.me, entry + 2]
            factor = jnp.where(c < counts[seg.me, t], scale(band), 0.0)
            prod = jnp.dot(
                ops[band, i], seg_buf[t, band * BLK_DEV + m], preferred_element_type=jnp.float32
            )
            prod = (prod * factor).astype(jnp.bfloat16)
            far[t, c, 0] = prod[:BLOCK]
            far[t, c, 1] = prod[BLOCK:]
        return carry

    lax.fori_loop(0, nseg, far_source, 0)

    seg.closing = grp.closing = True
    loop(begin)
    steps()


def body(nseg, ngrp, spectra, band_bins, far_list, far_count):
    cols = band_columns(spectra, band_bins)
    slots = far_list.shape[3]
    smem = pl.BlockSpec(memory_space=pltpu.SMEM)
    vmem = pl.BlockSpec(memory_space=pltpu.VMEM)
    sems = pltpu.SemaphoreType.DMA
    near, far = pl.pallas_call(
        functools.partial(kernel, nseg, ngrp),
        out_shape=(
            jax.ShapeDtypeStruct(
                (2, 2, BLK_DEV * BLOCK, ngrp * BLK_DEV * BLOCK), jnp.bfloat16
            ),
            jax.ShapeDtypeStruct((nseg, slots, 2, BLOCK, BLOCK), jnp.bfloat16),
        ),
        in_specs=[smem, smem, smem, vmem],
        out_specs=(vmem, vmem),
        scratch_shapes=[
            pltpu.VMEM((nseg, PIECES, DEPTH, BLOCK), jnp.bfloat16),
            pltpu.VMEM((ngrp, PIECES, DEPTH, BLOCK), jnp.bfloat16),
            pltpu.VMEM((2, BLK_DEV, 2 * BLOCK, DEPTH), jnp.bfloat16),
            sems((4, nseg, PIECES)),
            sems((nseg, PIECES)),
            sems((4, ngrp, PIECES)),
            sems((ngrp, PIECES)),
            sems,
        ],
        compiler_params=pltpu.CompilerParams(
            collective_id=0, has_side_effects=True, vmem_limit_bytes=56 * 1024 * 1024
        ),
    )(band_bins, far_list.reshape(nseg, nseg * slots * 3), far_count[0], cols)
    return (near, far[None, None])


def solution(mesh):
    placed = (
        P(None, None, None, ("seg", "grp")),
        P(),
        P("grp", None, None, None, None),
        P("grp", None, None),
    )
    return jax.shard_map(
        functools.partial(body, mesh.shape["seg"], mesh.shape["grp"]),
        mesh=mesh,
        in_specs=placed,
        out_specs=(
            P(None, None, ("seg", "grp"), None),
            P("seg", "grp", None, None, None, None, None),
        ),
        check_vma=False,
    )
```

```python
import functools

import jax
import jax.numpy as jnp
from jax import lax
from jax.experimental import pallas as pl
from jax.experimental.pallas import tpu as pltpu
from jax.sharding import PartitionSpec as P

W = 8
F = 128
BAND_MAX = 48
SMOOTH = 4
BLOCK = 128
BLK_DEV = 3
DEPTH = W * 2 * BAND_MAX
PIECES = 2 * BLK_DEV
LINE_Z = 4
CORES = 2


HIGH = lax.Precision.HIGHEST
MESH = pl.DeviceIdType.MESH


def whiten_kernel(bins, spectra, cols, gain):
    power = jnp.zeros((F, BLOCK), jnp.float32)
    for w in range(W):
        for p in range(2):
            values = spectra[w, p].astype(jnp.float32)
            power = power + values * values
    f = lax.broadcasted_iota(jnp.int32, (F, F), 0)
    g = lax.broadcasted_iota(jnp.int32, (F, F), 1)
    window = jnp.where(jnp.abs(f - g) <= SMOOTH, 1.0, 0.0).astype(jnp.float32)
    totals = jnp.sum(window, axis=1, keepdims=True) * W
    level = jnp.dot(window, power, precision=HIGH, preferred_element_type=jnp.float32) / totals
    gain[...] = lax.rsqrt(level + 1e-06)
    for band in range(2):
        at = pl.ds(pl.multiple_of(bins[band, 0], 16), BAND_MAX)
        scale = gain[at]
        for p in range(2):
            for w in range(W):
                first = (p * W + w) * BAND_MAX
                piece = spectra[w, p, at].astype(jnp.float32) * scale
                cols[band, 0, first : first + BAND_MAX] = piece.astype(jnp.bfloat16)


def band_columns(spectra, band_bins):
    return pl.pallas_call(
        whiten_kernel,
        grid=(BLK_DEV,),
        out_shape=jax.ShapeDtypeStruct((2, BLK_DEV, DEPTH, BLOCK), jnp.bfloat16),
        in_specs=[
            pl.BlockSpec(memory_space=pltpu.SMEM),
            pl.BlockSpec((W, 2, F, BLOCK), lambda m: (0, 0, 0, m)),
        ],
        out_specs=pl.BlockSpec((2, 1, DEPTH, BLOCK), lambda m: (0, m, 0, 0)),
        scratch_shapes=[pltpu.VMEM((F, BLOCK), jnp.float32)],
        compiler_params=pltpu.CompilerParams(vmem_limit_bytes=56 * 1024 * 1024),
    )(band_bins, spectra).reshape(PIECES, DEPTH, BLOCK)


class Gather:
    def __init__(self, axis, high, low, own, buf, send, recv):
        self.axis, self.high, self.low = axis, high, low
        self.own, self.buf, self.send, self.recv = own, buf, send, recv
        self.me = lax.axis_index(axis)
        self.p, self.l = lax.div(self.me, low), lax.rem(self.me, low)
        p, l = self.p, self.l
        self.dirs = [
            (p + 1 < high, self.me + low),
            (p > 0, self.me - low),
            (l + 1 < low, self.me + 1),
            (l > 0, self.me - 1),
        ]
        if high == 1:
            self.dirs[0] = self.dirs[1] = None
        if low == 1:
            self.dirs[2] = self.dirs[3] = None
        self.closing = False

    def greet(self, barrier):
        for entry in self.dirs:
            if entry is not None:

                @pl.when(entry[0])
                def _():
                    pl.semaphore_signal(
                        barrier, inc=1, device_id={self.axis: entry[1]}, device_id_type=MESH
                    )

    def peers(self):
        return sum(jnp.where(entry[0], 1, 0) for entry in self.dirs if entry is not None)

    def copy(self, way, src, q, own):
        return pltpu.make_async_remote_copy(
            src_ref=self.own.at[q] if own else self.buf.at[src, q],
            dst_ref=self.buf.at[src, q],
            send_sem=self.send.at[way, src, q],
            recv_sem=self.recv.at[src, q],
            device_id={self.axis: self.dirs[way][1]},
            device_id_type=MESH,
        )

    def pass_on(self, ways, src, q, own=False):
        for way in ways:
            if self.dirs[way] is not None:

                @pl.when(self.dirs[way][0])
                def _():
                    piece = self.copy(way, src, q, own)
                    if self.closing:
                        piece.wait_send()
                    else:
                        piece.start()

    def arrive(self, there, src, q, ways, use):
        @pl.when(there)
        def _():
            if not self.closing:
                pltpu.make_async_copy(
                    self.buf.at[src, q], self.buf.at[src, q], self.recv.at[src, q]
                ).wait()
            self.pass_on(ways, src, q)
            if use is not None and not self.closing:
                use(src, q)

    def start(self, q):
        self.pass_on((0, 1, 2, 3), self.me, q, own=True)

    def step(self, st, q, use, low_first=False):
        p, l, low = self.p, self.l, self.low
        turn = () if low_first else (2, 3)
        if 0 < st < self.high:
            self.arrive(p - st >= 0, (p - st) * low + l, q, (0,) + turn, use)
            self.arrive(p + st < self.high, (p + st) * low + l, q, (1,) + turn, use)
        d = st - 1
        if not 0 <= d < self.high:
            return
        for far, way in [(p, None)] if d == 0 else [(p - d, 0), (p + d, 1)]:
            inside = (far >= 0) & (far < self.high)
            for e in range(1, low):
                for there, other, on in ((l - e >= 0, l - e, 2), (l + e < low, l + e, 3)):
                    if not low_first:
                        ways = (on,)
                    elif d == 0:
                        ways = (0, 1, on)
                    else:
                        ways = (way,)
                    self.arrive(inside & there, far * low + other, q, ways, use)


def kernel(
    nseg, ngrp, bins, lists, counts, cols, near, far, seg_buf, grp_buf, ops,
    seg_send, seg_recv, grp_send, grp_recv, move,
):
    seg = Gather("seg", LINE_Z, nseg // LINE_Z, cols, seg_buf, seg_send, seg_recv)
    grp = Gather("grp", ngrp // CORES, CORES, cols, grp_buf, grp_send, grp_recv)
    barrier = pltpu.get_barrier_semaphore()
    seg.greet(barrier)
    grp.greet(barrier)
    pl.semaphore_wait(barrier, seg.peers() + grp.peers())

    def loop(fn, first=0):
        def step(q, carry):
            fn(q)
            return carry

        lax.fori_loop(first, PIECES, step, 0)

    def begin(q):
        seg.start(q)
        grp.start(q)

    loop(begin)
    own = pltpu.make_async_copy(cols, seg_buf.at[seg.me], move)
    own.start()

    half = DEPTH // 2

    def operands(q):
        band, m = lax.div(q, BLK_DEV), lax.rem(q, BLK_DEV)
        bin_of = lax.rem(lax.broadcasted_iota(jnp.int32, (1, DEPTH), 1), BAND_MAX)
        live = jnp.where(bin_of < bins[band, 1], 1.0, 0.0).astype(jnp.float32)
        rows = jnp.transpose(cols[q].astype(jnp.float32)) * live
        ops[band, m, :BLOCK] = rows.astype(jnp.bfloat16)
        ops[band, m, BLOCK:, :half] = rows[:, half:].astype(jnp.bfloat16)
        ops[band, m, BLOCK:, half:] = (-rows[:, :half]).astype(jnp.bfloat16)

    loop(operands)

    def scale(band):
        return lax.rsqrt(jnp.full((1, BLOCK), W * bins[band, 1], jnp.int32).astype(jnp.float32))

    def near_from(piece, src, q):
        band, m = lax.div(q, BLK_DEV), lax.rem(q, BLK_DEV)
        at = pl.ds(pl.multiple_of(src * (BLK_DEV * BLOCK) + m * BLOCK, BLOCK), BLOCK)
        for i in range(BLK_DEV):
            prod = jnp.dot(ops[band, i], piece, preferred_element_type=jnp.float32)
            prod = (prod * scale(band)).astype(jnp.bfloat16)
            near[band, 0, i * BLOCK : (i + 1) * BLOCK, at] = prod[:BLOCK]
            near[band, 1, i * BLOCK : (i + 1) * BLOCK, at] = prod[BLOCK:]

    def use_near(src, q):
        near_from(grp_buf[src, q], src, q)

    loop(lambda q: near_from(cols[q], grp.me, q))

    def steps():
        for st in range(1, max(seg.high, grp.high) + 1):

            def both(q, low_first=False):
                seg.step(st, q, None, low_first)
                grp.step(st, q, use_near)

            both(jnp.int32(0), low_first=True)
            loop(both, 1)

    steps()
    own.wait()

    slots = far.shape[1]

    def far_source(t, carry):
        for c in range(slots):
            entry = (t * slots + c) * 3
            i = lists[seg.me, entry]
            m = lists[seg.me, entry + 1]
            band = lists[seg.me, entry + 2]
            factor = jnp.where(c < counts[seg.me, t], scale(band), 0.0)
            prod = jnp.dot(
                ops[band, i], seg_buf[t, band * BLK_DEV + m], preferred_element_type=jnp.float32
            )
            prod = (prod * factor).astype(jnp.bfloat16)
            far[t, c, 0] = prod[:BLOCK]
            far[t, c, 1] = prod[BLOCK:]
        return carry

    lax.fori_loop(0, nseg, far_source, 0)

    seg.closing = grp.closing = True
    loop(begin)
    steps()


def body(nseg, ngrp, spectra, band_bins, far_list, far_count):
    cols = band_columns(spectra, band_bins)
    slots = far_list.shape[3]
    smem = pl.BlockSpec(memory_space=pltpu.SMEM)
    whole = pl.BlockSpec(memory_space=pltpu.VMEM)
    sems = pltpu.SemaphoreType.DMA
    shard = PIECES * DEPTH * BLOCK * 2
    result = (2 * 2 * BLK_DEV * BLOCK * ngrp * BLK_DEV + nseg * slots * 2 * BLOCK) * BLOCK * 2
    vmem = (nseg + ngrp + 4) * shard + result + 2 * 1024 * 1024
    near, far = pl.pallas_call(
        functools.partial(kernel, nseg, ngrp),
        out_shape=(
            jax.ShapeDtypeStruct(
                (2, 2, BLK_DEV * BLOCK, ngrp * BLK_DEV * BLOCK), jnp.bfloat16
            ),
            jax.ShapeDtypeStruct((nseg, slots, 2, BLOCK, BLOCK), jnp.bfloat16),
        ),
        in_specs=[smem, smem, smem, whole],
        out_specs=(whole, whole),
        scratch_shapes=[
            pltpu.VMEM((nseg, PIECES, DEPTH, BLOCK), jnp.bfloat16),
            pltpu.VMEM((ngrp, PIECES, DEPTH, BLOCK), jnp.bfloat16),
            pltpu.VMEM((2, BLK_DEV, 2 * BLOCK, DEPTH), jnp.bfloat16),
            sems((4, nseg, PIECES)),
            sems((nseg, PIECES)),
            sems((4, ngrp, PIECES)),
            sems((ngrp, PIECES)),
            sems,
        ],
        compiler_params=pltpu.CompilerParams(
            collective_id=0, has_side_effects=True, vmem_limit_bytes=vmem
        ),
    )(band_bins, far_list.reshape(nseg, nseg * slots * 3), far_count[0], cols)
    return (near, far[None, None])


def solution(mesh):
    placed = (
        P(None, None, None, ("seg", "grp")),
        P(),
        P("grp", None, None, None, None),
        P("grp", None, None),
    )
    return jax.shard_map(
        functools.partial(body, mesh.shape["seg"], mesh.shape["grp"]),
        mesh=mesh,
        in_specs=placed,
        out_specs=(
            P(None, None, ("seg", "grp"), None),
            P("seg", "grp", None, None, None, None, None),
        ),
        check_vma=False,
    )
```

```python
import functools

import jax
import jax.numpy as jnp
from jax import lax
from jax.experimental import pallas as pl
from jax.experimental.pallas import tpu as pltpu
from jax.sharding import PartitionSpec as P

W = 8
F = 128
BAND_MAX = 48
SMOOTH = 4
BLOCK = 128
BLK_DEV = 3
DEPTH = W * 2 * BAND_MAX
PIECES = 2 * BLK_DEV
LINE_Z = 4
GROUP = 8
GROUP_ROWS = W * 2 * GROUP
SIZES = (4, 5, 6)
CORES = 2


HIGH = lax.Precision.HIGHEST
MESH = pl.DeviceIdType.MESH


def whiten_kernel(bins, spectra, cols, gain):
    power = jnp.zeros((F, BLOCK), jnp.float32)
    for w in range(W):
        for p in range(2):
            values = spectra[w, p].astype(jnp.float32)
            power = power + values * values
    f = lax.broadcasted_iota(jnp.int32, (F, F), 0)
    g = lax.broadcasted_iota(jnp.int32, (F, F), 1)
    window = jnp.where(jnp.abs(f - g) <= SMOOTH, 1.0, 0.0).astype(jnp.float32)
    totals = jnp.sum(window, axis=1, keepdims=True) * W
    level = jnp.dot(window, power, precision=HIGH, preferred_element_type=jnp.float32) / totals
    gain[...] = lax.rsqrt(level + 1e-06)
    for band in range(2):
        at = pl.ds(pl.multiple_of(bins[band, 0], 16), BAND_MAX)
        scale = gain[at]
        for p in range(2):
            for w in range(0, W, 2):
                pair = [spectra[w + k, p, at].astype(jnp.float32) * scale for k in range(2)]
                for g in range(BAND_MAX // GROUP):
                    first = g * GROUP_ROWS + (p * W + w) * GROUP
                    rows = [v[g * GROUP : (g + 1) * GROUP] for v in pair]
                    rows = jnp.concatenate(rows, axis=0).astype(jnp.bfloat16)
                    cols[band, 0, first : first + 2 * GROUP] = rows


def band_columns(spectra, band_bins):
    return pl.pallas_call(
        whiten_kernel,
        grid=(BLK_DEV,),
        out_shape=jax.ShapeDtypeStruct((2, BLK_DEV, DEPTH, BLOCK), jnp.bfloat16),
        in_specs=[
            pl.BlockSpec(memory_space=pltpu.SMEM),
            pl.BlockSpec((W, 2, F, BLOCK), lambda m: (0, 0, 0, m)),
        ],
        out_specs=pl.BlockSpec((2, 1, DEPTH, BLOCK), lambda m: (0, m, 0, 0)),
        scratch_shapes=[pltpu.VMEM((F, BLOCK), jnp.float32)],
        compiler_params=pltpu.CompilerParams(vmem_limit_bytes=56 * 1024 * 1024),
    )(band_bins, spectra).reshape(PIECES, DEPTH, BLOCK)


class Gather:
    def __init__(self, axis, high, low, own, buf, send, recv):
        self.axis, self.high, self.low = axis, high, low
        self.own, self.buf, self.send, self.recv = own, buf, send, recv
        self.me = lax.axis_index(axis)
        self.p, self.l = lax.div(self.me, low), lax.rem(self.me, low)
        p, l = self.p, self.l
        self.dirs = [
            (p + 1 < high, self.me + low),
            (p > 0, self.me - low),
            (l + 1 < low, self.me + 1),
            (l > 0, self.me - 1),
        ]
        if high == 1:
            self.dirs[0] = self.dirs[1] = None
        if low == 1:
            self.dirs[2] = self.dirs[3] = None
        self.closing = False
        self.rows = DEPTH

    def greet(self, barrier):
        for entry in self.dirs:
            if entry is not None:

                @pl.when(entry[0])
                def _():
                    pl.semaphore_signal(
                        barrier, inc=1, device_id={self.axis: entry[1]}, device_id_type=MESH
                    )

    def peers(self):
        return sum(jnp.where(entry[0], 1, 0) for entry in self.dirs if entry is not None)

    def copy(self, way, src, q, own):
        return pltpu.make_async_remote_copy(
            src_ref=self.own.at[q, : self.rows] if own else self.buf.at[src, q, : self.rows],
            dst_ref=self.buf.at[src, q, : self.rows],
            send_sem=self.send.at[way, src, q],
            recv_sem=self.recv.at[src, q],
            device_id={self.axis: self.dirs[way][1]},
            device_id_type=MESH,
        )

    def pass_on(self, ways, src, q, own=False):
        for way in ways:
            if self.dirs[way] is not None:

                @pl.when(self.dirs[way][0])
                def _():
                    piece = self.copy(way, src, q, own)
                    if self.closing:
                        piece.wait_send()
                    else:
                        piece.start()

    def arrive(self, there, src, q, ways, use):
        @pl.when(there)
        def _():
            if not self.closing:
                piece = self.buf.at[src, q, : self.rows]
                pltpu.make_async_copy(piece, piece, self.recv.at[src, q]).wait()
            self.pass_on(ways, src, q)
            if use is not None and not self.closing:
                use(src, q)

    def start(self, q):
        self.pass_on((0, 1, 2, 3), self.me, q, own=True)

    def step(self, st, q, use, low_first=False):
        p, l, low = self.p, self.l, self.low
        turn = () if low_first else (2, 3)
        if 0 < st < self.high:
            self.arrive(p - st >= 0, (p - st) * low + l, q, (0,) + turn, use)
            self.arrive(p + st < self.high, (p + st) * low + l, q, (1,) + turn, use)
        d = st - 1
        if not 0 <= d < self.high:
            return
        for far, way in [(p, None)] if d == 0 else [(p - d, 0), (p + d, 1)]:
            inside = (far >= 0) & (far < self.high)
            for e in range(1, low):
                for there, other, on in ((l - e >= 0, l - e, 2), (l + e < low, l + e, 3)):
                    if not low_first:
                        ways = (on,)
                    elif d == 0:
                        ways = (0, 1, on)
                    else:
                        ways = (way,)
                    self.arrive(inside & there, far * low + other, q, ways, use)


def kernel(
    nseg, ngrp, groups, bins, lists, counts, cols, near, far, seg_buf, grp_buf, ops,
    seg_send, seg_recv, grp_send, grp_recv, move,
):
    seg = Gather("seg", LINE_Z, nseg // LINE_Z, cols, seg_buf, seg_send, seg_recv)
    grp = Gather("grp", ngrp // CORES, CORES, cols, grp_buf, grp_send, grp_recv)
    short = groups * GROUP_ROWS
    if short < DEPTH:

        def clear(t, carry):
            seg_buf[t, BLK_DEV:, short:] = jnp.zeros(
                (BLK_DEV, DEPTH - short, BLOCK), jnp.bfloat16
            )
            return carry

        lax.fori_loop(0, nseg, clear, 0)

    barrier = pltpu.get_barrier_semaphore()
    seg.greet(barrier)
    grp.greet(barrier)
    pl.semaphore_wait(barrier, seg.peers() + grp.peers())

    def loop(fn, first=0):
        def step(q, carry):
            fn(q)
            return carry

        for low, high, rows in ((first, BLK_DEV, DEPTH), (BLK_DEV, PIECES, short)):
            seg.rows = grp.rows = rows
            lax.fori_loop(low, high, step, 0)
        seg.rows = grp.rows = DEPTH

    def begin(q):
        seg.start(q)
        grp.start(q)

    loop(begin)
    own = pltpu.make_async_copy(cols, seg_buf.at[seg.me], move)
    own.start()

    def operands(q):
        band, m = lax.div(q, BLK_DEV), lax.rem(q, BLK_DEV)
        row = lax.broadcasted_iota(jnp.int32, (DEPTH, BLOCK), 0)
        bin_of = lax.div(row, GROUP_ROWS) * GROUP + lax.rem(row, GROUP)
        live = jnp.where(bin_of < bins[band, 1], 1.0, 0.0).astype(jnp.float32)
        rows = cols[q].astype(jnp.float32) * live
        turned = []
        for g in range(0, DEPTH, GROUP_ROWS):
            turned.append(rows[g + GROUP_ROWS // 2 : g + GROUP_ROWS])
            turned.append(-rows[g : g + GROUP_ROWS // 2])
        ops[band, m, :BLOCK] = jnp.transpose(rows).astype(jnp.bfloat16)
        ops[band, m, BLOCK:] = jnp.transpose(jnp.concatenate(turned, axis=0)).astype(jnp.bfloat16)

    loop(operands)

    def scale(band):
        return lax.rsqrt(jnp.full((1, BLOCK), W * bins[band, 1], jnp.int32).astype(jnp.float32))

    def near_from(piece, src, q):
        band, m = lax.div(q, BLK_DEV), lax.rem(q, BLK_DEV)
        at = pl.ds(pl.multiple_of(src * (BLK_DEV * BLOCK) + m * BLOCK, BLOCK), BLOCK)
        for i in range(BLK_DEV):
            prod = jnp.dot(ops[band, i, :, : grp.rows], piece, preferred_element_type=jnp.float32)
            prod = (prod * scale(band)).astype(jnp.bfloat16)
            near[band, 0, i * BLOCK : (i + 1) * BLOCK, at] = prod[:BLOCK]
            near[band, 1, i * BLOCK : (i + 1) * BLOCK, at] = prod[BLOCK:]

    def use_near(src, q):
        near_from(grp_buf[src, q, : grp.rows], src, q)

    loop(lambda q: near_from(cols[q, : grp.rows], grp.me, q))

    def steps():
        for st in range(1, max(seg.high, grp.high) + 1):

            def both(q, low_first=False):
                seg.step(st, q, None, low_first)
                grp.step(st, q, use_near)

            both(jnp.int32(0), low_first=True)
            loop(both, 1)

    steps()
    own.wait()

    slots = far.shape[1]

    def far_source(t, carry):
        for c in range(slots):
            entry = (t * slots + c) * 3
            i = lists[seg.me, entry]
            m = lists[seg.me, entry + 1]
            band = lists[seg.me, entry + 2]
            factor = jnp.where(c < counts[seg.me, t], scale(band), 0.0)
            prod = jnp.dot(
                ops[band, i], seg_buf[t, band * BLK_DEV + m], preferred_element_type=jnp.float32
            )
            prod = (prod * factor).astype(jnp.bfloat16)
            far[t, c, 0] = prod[:BLOCK]
            far[t, c, 1] = prod[BLOCK:]
        return carry

    lax.fori_loop(0, nseg, far_source, 0)

    seg.closing = grp.closing = True
    loop(begin)
    steps()


def body(nseg, ngrp, spectra, band_bins, far_list, far_count):
    cols = band_columns(spectra, band_bins)
    slots = far_list.shape[3]
    smem = pl.BlockSpec(memory_space=pltpu.SMEM)
    whole = pl.BlockSpec(memory_space=pltpu.VMEM)
    sems = pltpu.SemaphoreType.DMA
    shard = PIECES * DEPTH * BLOCK * 2
    result = (2 * 2 * BLK_DEV * BLOCK * ngrp * BLK_DEV + nseg * slots * 2 * BLOCK) * BLOCK * 2
    vmem = (nseg + ngrp + 4) * shard + result + 2 * 1024 * 1024
    def with_groups(groups, *arrays):
        return pl.pallas_call(
            functools.partial(kernel, nseg, ngrp, groups),
            out_shape=(
                jax.ShapeDtypeStruct(
                    (2, 2, BLK_DEV * BLOCK, ngrp * BLK_DEV * BLOCK), jnp.bfloat16
                ),
                jax.ShapeDtypeStruct((nseg, slots, 2, BLOCK, BLOCK), jnp.bfloat16),
            ),
            in_specs=[smem, smem, smem, whole],
            out_specs=(whole, whole),
            scratch_shapes=[
                pltpu.VMEM((nseg, PIECES, DEPTH, BLOCK), jnp.bfloat16),
                pltpu.VMEM((ngrp, PIECES, DEPTH, BLOCK), jnp.bfloat16),
                pltpu.VMEM((2, BLK_DEV, 2 * BLOCK, DEPTH), jnp.bfloat16),
                sems((4, nseg, PIECES)),
                sems((nseg, PIECES)),
                sems((4, ngrp, PIECES)),
                sems((ngrp, PIECES)),
                sems,
            ],
            compiler_params=pltpu.CompilerParams(
                collective_id=groups, has_side_effects=True, vmem_limit_bytes=vmem
            ),
        )(*arrays)

    arrays = (band_bins, far_list.reshape(nseg, nseg * slots * 3), far_count[0], cols)
    needed = (band_bins[1, 1] + GROUP - 1) // GROUP
    near, far = lax.switch(
        jnp.clip(needed - SIZES[0], 0, len(SIZES) - 1),
        [functools.partial(with_groups, groups) for groups in SIZES],
        *arrays,
    )
    return (near, far[None, None])


def solution(mesh):
    placed = (
        P(None, None, None, ("seg", "grp")),
        P(),
        P("grp", None, None, None, None),
        P("grp", None, None),
    )
    return jax.shard_map(
        functools.partial(body, mesh.shape["seg"], mesh.shape["grp"]),
        mesh=mesh,
        in_specs=placed,
        out_specs=(
            P(None, None, ("seg", "grp"), None),
            P("seg", "grp", None, None, None, None, None),
        ),
        check_vma=False,
    )
```
